32 devices in a mesh: dp: 4 (over z), fsdp: 8 (over y, x, core).
Axes of the slice: x: 2, y: 2, z: 4, core: 2. Of those that a mesh axis runs over, the one named last changes fastest.
Arguments:
- tokens: bfloat16 [128, 8192], P('dp', 'fsdp'), may hold values from -6 to 6
- cotangent: bfloat16 [128, 8192], P('dp', 'fsdp'), may hold values from -6 to 6
- w_gate: bfloat16 [16384, 8192], P(('dp', 'fsdp')), may hold values from -0.0625 to 0.0625
- w_up: bfloat16 [16384, 8192], P(('dp', 'fsdp')), may hold values from -0.0625 to 0.0625
- w_down: bfloat16 [16384, 8192], P(('dp', 'fsdp')), may hold values from -0.046875 to 0.046875
- t_gate: bfloat16 [16384, 8192], P(('dp', 'fsdp')), may hold values from -0.0625 to 0.0625
- t_up: bfloat16 [16384, 8192], P(('dp', 'fsdp')), may hold values from -0.0625 to 0.0625
Outputs:
- hvp_gate: float32 [16384, 8192], P(('dp', 'fsdp'))
- hvp_up: float32 [16384, 8192], P(('dp', 'fsdp'))
The draws below stay inside these ranges and needn't reach their ends.
All inputs are finite; a program needn't handle non-finite values.
Results may differ from the reference program's by a relative error of at most 0.003.
Values may be sent and summed in bfloat16 or wider, within the bound.
A program may use at most 192 MiB of HBM per device.

```python
import math
import jax
import jax.numpy as jnp

D = 8192
FF = 16384
TOKENS = 128


def block_scale(stream_key, shape, cuts, low, top_value):
    def one(dim, parts):
        steps = jax.random.uniform(jax.random.fold_in(jax.random.fold_in(stream_key, 6), dim), (parts,), jnp.float32, low / len(cuts), top_value / len(cuts))
        return jnp.repeat(jnp.exp(steps), shape[dim] // parts).reshape((-1,) + (1,) * (len(shape) - dim - 1))

    loudness = one(*cuts[0])
    for cut in cuts[1:]:
        loudness = loudness * one(*cut)
    return loudness


def gaussian(key, extent, width, reach, shards=(), held_as=jnp.bfloat16):
    loudness = block_scale(key, extent, shards, -0.22, 0.18) if shards else 1.0
    entries = jax.random.normal(key, extent, jnp.float32) * width * loudness
    return jnp.minimum(jnp.maximum(entries, -reach), reach).astype(held_as)


def setup_inputs(seed: int = 0) -> dict:
    keys = jax.random.split(jax.random.key(seed), 8)
    tokens = gaussian(keys[0], (TOKENS, D), 1.0, 6.0, ((0, 4), (1, 8)))
    cotangent = gaussian(keys[1], (TOKENS, D), 1.0, 6.0, ((0, 4), (1, 8)))
    w_gate = gaussian(keys[2], (FF, D), D ** -0.5, 0.0625, ((0, 32),))
    w_up = gaussian(keys[3], (FF, D), D ** -0.5, 0.0625, ((0, 32),))
    w_down = gaussian(keys[4], (FF, D), FF ** -0.5, 0.046875, ((0, 32),))
    t_gate = gaussian(keys[5], (FF, D), D ** -0.5, 0.0625, ((0, 32),))
    t_up = gaussian(keys[6], (FF, D), D ** -0.5, 0.0625, ((0, 32),))
    return {"tokens": tokens, "cotangent": cotangent, "w_gate": w_gate, "w_up": w_up, "w_down": w_down, "t_gate": t_gate, "t_up": t_up}


def reference(tokens, cotangent, w_gate, w_up, w_down, t_gate, t_up):
    gate = jnp.dot(tokens, w_gate.T, preferred_element_type=jnp.float32)
    up = jnp.dot(tokens, w_up.T, preferred_element_type=jnp.float32)
    gate_dot = jnp.dot(tokens, t_gate.T, preferred_element_type=jnp.float32)
    up_dot = jnp.dot(tokens, t_up.T, preferred_element_type=jnp.float32)
    back = jnp.dot(cotangent, w_down.T, preferred_element_type=jnp.float32)
    sigmoid_gate = jax.nn.sigmoid(gate)
    first = sigmoid_gate * (1.0 + gate * (1.0 - sigmoid_gate))
    second = sigmoid_gate * (1.0 - sigmoid_gate) * (2.0 + gate * (1.0 - 2.0 * sigmoid_gate))
    factor_gate = (back * (up_dot * first + up * second * gate_dot)).astype(jnp.bfloat16)
    factor_up = (back * first * gate_dot).astype(jnp.bfloat16)
    scale = 1.0 / math.sqrt(TOKENS)
    hvp_gate = jnp.dot(factor_gate.T, tokens, preferred_element_type=jnp.float32) * scale
    hvp_up = jnp.dot(factor_up.T, tokens, preferred_element_type=jnp.float32) * scale
    return (hvp_gate, hvp_up)
```

```python
import functools
import math

import jax
import jax.numpy as jnp
from jax import lax
from jax.experimental import pallas as pl
from jax.experimental.pallas import tpu as pltpu
from jax.sharding import PartitionSpec as P

MESH = pl.DeviceIdType.MESH


def contract(weight, block):
    return lax.dot_general(
        weight, block, (((1,), (1,)), ((), ())), preferred_element_type=jnp.float32
    )


def factors(gate, up, gate_dot, up_dot, back):
    s = jax.nn.sigmoid(gate)
    first = s * (1.0 + gate * (1.0 - s))
    second = s * (1.0 - s) * (2.0 + gate * (1.0 - 2.0 * s))
    factor_gate = (back * (up_dot * first + up * second * gate_dot)).astype(jnp.bfloat16)
    factor_up = (back * first * gate_dot).astype(jnp.bfloat16)
    return factor_gate, factor_up


def gather_kernel(
    tok_hbm, cot_hbm, wg, wu, tg, tu, wd,
    fg_out, fu_out, tok_out,
    w4, wdn, buf, acc, accb,
    wsem, dsem, isem, osem,
    zs, zr, xs, xr, ys, yr, dxs, dxr, dys, dyr, ss, sr,
):
    rows, cols = tok_hbm.shape
    hidden = wg.shape[0]
    half = rows // 2
    z = lax.axis_index("dp")
    f = lax.axis_index("fsdp")
    core = f % 2
    q = f // 2
    x = q % 2
    y = q // 2

    def feat(yy, xx, cc):
        return (yy * 2 + xx) * 2 + cc

    fx = feat(y, 1 - x, core)
    fy = feat(1 - y, x, core)
    fs = feat(y, x, 1 - core)
    fidx = [feat(yy, xx, cc) for cc in (core, 1 - core)
            for yy, xx in ((y, x), (y, 1 - x), (1 - y, x), (1 - y, 1 - x))]
    zi = [z, z + 1 - 2 * (z % 2), (z + 2) % 4, 3 - z]

    inputs = [pltpu.make_async_copy(src, buf.at[t, 0, pl.ds(0, rows)], isem.at[t])
              for t, src in enumerate((tok_hbm, cot_hbm))]
    for c in inputs:
        c.start()

    barrier = pltpu.get_barrier_semaphore()
    partners = [(zi[1], f), (zi[2], f), (zi[3], f), (z, fx), (z, fy), (z, fs)]
    for who in partners:
        pl.semaphore_signal(barrier, inc=1, device_id=who, device_id_type=MESH)

    loads = []
    for p in range(8):
        loads.append([
            pltpu.make_async_copy(
                src.at[:, pl.ds(pl.multiple_of(fidx[p] * cols, cols), cols)],
                w4.at[p, pl.ds(w * hidden, hidden)], wsem.at[p, w])
            for w, src in enumerate((wg, wu, tg, tu))])
    dloads = [
        pltpu.make_async_copy(
            wd.at[:, pl.ds(pl.multiple_of(fidx[p] * cols, cols), cols)],
            wdn.at[p], dsem.at[p])
        for p in range(8)]
    for group in loads:
        for c in group:
            c.start()
    for c in dloads:
        c.start()

    def remote(t, p_src, p_dst, r_src, r_dst, n, send, recv, who):
        return pltpu.make_async_remote_copy(
            src_ref=buf.at[t, p_src, pl.ds(r_src, n)],
            dst_ref=buf.at[t, p_dst, pl.ds(r_dst, n)],
            send_sem=send, recv_sem=recv, device_id=who, device_id_type=MESH)

    def zcopy(t, i):
        return remote(t, 0, 0, 0, i * rows, rows, zs.at[t, i], zr.at[t, i], (zi[i], f))

    def xcopy(t, i):
        return remote(t, 0, 1, i * rows, i * rows, rows, xs.at[t, i], xr.at[t, i], (z, fx))

    def ycopy(t, i):
        return remote(t, 0, 2, i * rows, i * rows, rows, ys.at[t, i], yr.at[t, i], (z, fy))

    def dycopy(t, i):
        return remote(t, 1, 3, i * rows, i * rows, half, dys.at[t, i], dyr.at[t, i], (z, fy))

    def dxcopy(t, i):
        r = i * rows + half
        return remote(t, 2, 3, r, r, half, dxs.at[t, i], dxr.at[t, i], (z, fx))

    def scopy(t, p, h):
        r = h * 2 * rows
        return remote(t, p, 4 + p, r, r, 2 * rows, ss.at[t, p, h], sr.at[t, p, h], (z, fs))

    def own_z(t):
        for i in (1, 2, 3):
            zcopy(t, i).start()

    def own_xy(t):
        xcopy(t, 0).start()
        ycopy(t, 0).start()

    def pass_z(t, i):
        zcopy(t, i).wait_recv()
        xcopy(t, i).start()
        ycopy(t, i).start()
        if i % 2 == 1:
            scopy(t, 0, i // 2).start()

    def pass_xy(t, i):
        xcopy(t, i).wait_recv()
        dycopy(t, i).start()
        ycopy(t, i).wait_recv()
        dxcopy(t, i).start()
        if i % 2 == 1:
            scopy(t, 1, i // 2).start()
            scopy(t, 2, i // 2).start()

    def pass_d(t, h):
        for i in (2 * h, 2 * h + 1):
            dycopy(t, i).wait_recv()
            dxcopy(t, i).wait_recv()
        scopy(t, 3, h).start()

    def ready_sib(t, p):
        if p >= 4:
            scopy(t, p - 4, 0).wait_recv()
            scopy(t, p - 4, 1).wait_recv()

    out_copies = [pltpu.make_async_copy(buf.at[0, p], tok_out.at[fidx[p]], osem.at[p])
                  for p in range(8)]

    def dots(p, part):
        for w in (2 * part, 2 * part + 1):
            loads[p][w].wait()

        def body(k, carry):
            r = pl.ds(pl.multiple_of(k * hidden, hidden), hidden)
            d = contract(w4[p, r], buf[0, p])
            if p == 0:
                acc[r] = d
            else:
                acc[r] += d
            return carry
        lax.fori_loop(2 * part, 2 * part + 2, body, 0)

    for c in inputs:
        c.wait()
    pl.semaphore_wait(barrier, len(partners))

    own_z(0)
    own_xy(0)
    pass_z(0, 1)
    pass_xy(0, 0)
    pass_z(0, 2)
    pass_xy(0, 1)
    pass_z(0, 3)
    own_z(1)
    pass_d(0, 0)
    pass_xy(0, 2)
    own_xy(1)
    pass_xy(0, 3)
    pass_d(0, 1)

    def step(p, first=None, second=None):
        ready_sib(0, p)
        out_copies[p].start()
        dots(p, 0)
        if first is not None:
            first()
        dots(p, 1)
        if second is not None:
            second()

    step(0, lambda: pass_z(1, 1))
    step(1, lambda: pass_xy(1, 0))
    step(2, lambda: pass_z(1, 2))
    step(3, lambda: pass_xy(1, 1), lambda: pass_z(1, 3))
    step(4, lambda: pass_d(1, 0))
    step(5, lambda: pass_xy(1, 2))
    step(6)
    step(7, lambda: pass_xy(1, 3))


    def back(p):
        ready_sib(1, p)
        dloads[p].wait()
        d = contract(wdn[p], buf[1, p])
        if p == 0:
            accb[...] = d
        else:
            accb[...] += d

    back(0)
    pass_d(1, 1)
    for p in (1, 2, 3, 4, 5, 6, 7):
        back(p)

    chunk = hidden // 4

    def finish(k, carry):
        def part(w):
            return acc[pl.ds(pl.multiple_of(w * hidden + k * chunk, chunk), chunk)]
        r = pl.ds(pl.multiple_of(k * chunk, chunk), chunk)
        fg, fu = factors(part(0), part(1), part(2), part(3), accb[r])
        fg_out[r] = fg
        fu_out[r] = fu
        return carry
    lax.fori_loop(0, 4, finish, 0)

    for c in out_copies:
        c.wait()
    for t in (0, 1):
        for i in (1, 2, 3):
            zcopy(t, i).wait_send()
        for i in range(4):
            xcopy(t, i).wait_send()
            ycopy(t, i).wait_send()
            dxcopy(t, i).wait_send()
            dycopy(t, i).wait_send()
        for p in range(4):
            for h in (0, 1):
                scopy(t, p, h).wait_send()


def outer_kernel(scale, fg, fu, tok, og, ou):
    t = tok[0]
    og[...] = jnp.dot(fg[...], t, preferred_element_type=jnp.float32) * scale
    ou[...] = jnp.dot(fu[...], t, preferred_element_type=jnp.float32) * scale


def local_kernels(tokens, cotangent, w_gate, w_up, w_down, t_gate, t_up):
    n_dp, n_fs = lax.axis_size("dp"), lax.axis_size("fsdp")
    rows, cols = tokens.shape
    hidden, width = w_gate.shape
    total = rows * n_dp
    scale = 1.0 / math.sqrt(total)
    anywhere = pl.BlockSpec(memory_space=pl.ANY)
    vmem = pl.BlockSpec(memory_space=pltpu.VMEM)
    dma = pltpu.SemaphoreType.DMA
    fg, fu, tok = pl.pallas_call(
        gather_kernel,
        out_shape=(
            jax.ShapeDtypeStruct((hidden, total), jnp.bfloat16),
            jax.ShapeDtypeStruct((hidden, total), jnp.bfloat16),
            jax.ShapeDtypeStruct((n_fs, total, cols), jnp.bfloat16),
        ),
        in_specs=[anywhere] * 7,
        out_specs=(vmem, vmem, anywhere),
        scratch_shapes=[
            pltpu.VMEM((n_fs, 4 * hidden, cols), jnp.bfloat16),
            pltpu.VMEM((n_fs, hidden, cols), jnp.bfloat16),
            pltpu.VMEM((2, n_fs, total, cols), jnp.bfloat16),
            pltpu.VMEM((4 * hidden, total), jnp.float32),
            pltpu.VMEM((hidden, total), jnp.float32),
            dma((8, 4)), dma((8,)), dma((2,)), dma((8,)),
        ] + [dma((2, 4))] * 10 + [dma((2, 4, 2))] * 2,
        compiler_params=pltpu.CompilerParams(
            collective_id=0, has_side_effects=True, vmem_limit_bytes=56 * 2**20),
        cost_estimate=pl.CostEstimate(
            flops=10 * hidden * width * total, bytes_accessed=10 * hidden * width,
            transcendentals=hidden * total),
        name="gather_factors",
    )(tokens, cotangent, w_gate, w_up, t_gate, t_up, w_down)
    whole = pl.BlockSpec((hidden, total), lambda j: (0, 0))
    out = pl.BlockSpec((hidden, cols), lambda j: (0, j))
    return pl.pallas_call(
        functools.partial(outer_kernel, scale),
        grid=(n_fs,),
        out_shape=(jax.ShapeDtypeStruct((hidden, width), jnp.float32),) * 2,
        in_specs=[whole, whole, pl.BlockSpec((1, total, cols), lambda j: (j, 0, 0))],
        out_specs=(out, out),
        compiler_params=pltpu.CompilerParams(vmem_limit_bytes=32 * 2**20),
        cost_estimate=pl.CostEstimate(
            flops=4 * hidden * width * total, bytes_accessed=8 * hidden * width,
            transcendentals=0),
        name="outer",
    )(fg, fu, tok)


def local(tokens, cotangent, w_gate, w_up, w_down, t_gate, t_up):
    scale = 1.0 / math.sqrt(tokens.shape[0] * lax.axis_size("dp"))
    full_tok, full_cot = (
        lax.all_gather(lax.all_gather(a, "fsdp", axis=1, tiled=True), "dp", axis=0, tiled=True)
        for a in (tokens, cotangent)
    )
    factor_gate, factor_up = factors(
        *(contract(w, full_tok) for w in (w_gate, w_up, t_gate, t_up)),
        contract(w_down, full_cot),
    )
    return tuple(
        jnp.dot(a, full_tok, preferred_element_type=jnp.float32) * scale
        for a in (factor_gate, factor_up)
    )


def solution(mesh):
    spec = P("dp", "fsdp")
    weight = P(("dp", "fsdp"), None)
    square = mesh.shape["dp"] == 4 and mesh.shape["fsdp"] == 8
    return jax.shard_map(
        local_kernels if square else local, mesh=mesh,
        in_specs=(spec,) * 2 + (weight,) * 5, out_specs=(weight,) * 2, check_vma=False)
```

```python
import functools
import math

import jax
import jax.numpy as jnp
from jax import lax
from jax.experimental import pallas as pl
from jax.experimental.pallas import tpu as pltpu
from jax.sharding import PartitionSpec as P

MESH = pl.DeviceIdType.MESH


def contract(weight, block):
    return lax.dot_general(
        weight, block, (((1,), (1,)), ((), ())), preferred_element_type=jnp.float32
    )


def factors(gate, up, gate_dot, up_dot, back):
    s = jax.nn.sigmoid(gate)
    first = s * (1.0 + gate * (1.0 - s))
    second = s * (1.0 - s) * (2.0 + gate * (1.0 - 2.0 * s))
    factor_gate = (back * (up_dot * first + up * second * gate_dot)).astype(jnp.bfloat16)
    factor_up = (back * first * gate_dot).astype(jnp.bfloat16)
    return factor_gate, factor_up


def gather_kernel(
    tok_hbm, cot_hbm, wg, wu, tg, tu, wd,
    fg_out, fu_out, tok_out,
    w4, wdn, buf, acc, accb,
    wsem, dsem, isem, osem,
    zs, zr, xs, xr, ys, yr, dxs, dxr, dys, dyr, ss, sr,
):
    rows, cols = tok_hbm.shape
    hidden = wg.shape[0]
    half = rows // 2
    z = lax.axis_index("dp")
    f = lax.axis_index("fsdp")
    core = f % 2
    q = f // 2
    x = q % 2
    y = q // 2

    def feat(yy, xx, cc):
        return (yy * 2 + xx) * 2 + cc

    fx = feat(y, 1 - x, core)
    fy = feat(1 - y, x, core)
    fd = feat(1 - y, 1 - x, core)
    fs = feat(y, x, 1 - core)
    fidx = [feat(yy, xx, cc) for cc in (core, 1 - core)
            for yy, xx in ((y, x), (y, 1 - x), (1 - y, x), (1 - y, 1 - x))]
    zi = [z, z + 1 - 2 * (z % 2), (z + 2) % 4, 3 - z]

    inputs = [pltpu.make_async_copy(src, buf.at[t, 0, pl.ds(0, rows)], isem.at[t])
              for t, src in enumerate((tok_hbm, cot_hbm))]
    for c in inputs:
        c.start()

    barrier = pltpu.get_barrier_semaphore()
    partners = [(zi[1], f), (zi[2], f), (zi[3], f), (z, fx), (z, fy), (z, fd), (z, fs)]
    for who in partners:
        pl.semaphore_signal(barrier, inc=1, device_id=who, device_id_type=MESH)

    loads = []
    for p in range(8):
        loads.append([
            pltpu.make_async_copy(
                src.at[:, pl.ds(pl.multiple_of(fidx[p] * cols, cols), cols)],
                w4.at[p, pl.ds(w * hidden, hidden)], wsem.at[p, w])
            for w, src in enumerate((wg, wu, tg, tu))])
    dloads = [
        pltpu.make_async_copy(
            wd.at[:, pl.ds(pl.multiple_of(fidx[p] * cols, cols), cols)],
            wdn.at[p], dsem.at[p])
        for p in range(8)]
    order = (0, 4, 1, 2, 5, 6, 3, 7)
    for p in order:
        for c in loads[p]:
            c.start()
    for p in order:
        dloads[p].start()

    def remote(t, p_src, p_dst, r_src, r_dst, n, send, recv, who):
        return pltpu.make_async_remote_copy(
            src_ref=buf.at[t, p_src, pl.ds(r_src, n)],
            dst_ref=buf.at[t, p_dst, pl.ds(r_dst, n)],
            send_sem=send, recv_sem=recv, device_id=who, device_id_type=MESH)

    def zcopy(t, i):
        return remote(t, 0, 0, 0, i * rows, rows, zs.at[t, i], zr.at[t, i], (zi[i], f))

    def xcopy(t, i):
        return remote(t, 0, 1, i * rows, i * rows, rows, xs.at[t, i], xr.at[t, i], (z, fx))

    def ycopy(t, i):
        return remote(t, 0, 2, i * rows, i * rows, rows, ys.at[t, i], yr.at[t, i], (z, fy))

    def dycopy(t, i):
        return remote(t, 1, 3, i * rows, i * rows, half, dys.at[t, i], dyr.at[t, i], (z, fy))

    def dxcopy(t, i):
        r = i * rows + half
        return remote(t, 2, 3, r, r, half, dxs.at[t, i], dxr.at[t, i], (z, fx))

    def dcopy(i):
        return remote(1, 0, 3, i * rows, i * rows, rows, dxs.at[1, i], dxr.at[1, i], (z, fd))

    def scopy(t, p, h):
        r = h * 2 * rows
        return remote(t, p, 4 + p, r, r, 2 * rows, ss.at[t, p, h], sr.at[t, p, h], (z, fs))

    def across(t, i):
        xcopy(t, i).start()
        ycopy(t, i).start()
        if t == 1:
            dcopy(i).start()

    def pass_z(t, i):
        zcopy(t, i).wait_recv()
        across(t, i)
        if i % 2 == 1:
            scopy(t, 0, i // 2).start()

    def sib(p, h):
        for i in (2 * h, 2 * h + 1):
            {1: lambda: xcopy(1, i), 2: lambda: ycopy(1, i), 3: lambda: dcopy(i)}[p]().wait_recv()
        scopy(1, p, h).start()

    def pass_xy(t, i):
        xcopy(t, i).wait_recv()
        dycopy(t, i).start()
        ycopy(t, i).wait_recv()
        dxcopy(t, i).start()
        if i % 2 == 1:
            scopy(t, 1, i // 2).start()
            scopy(t, 2, i // 2).start()

    def pass_d(t, h):
        for i in (2 * h, 2 * h + 1):
            dycopy(t, i).wait_recv()
            dxcopy(t, i).wait_recv()
        scopy(t, 3, h).start()

    def ready_sib(t, p):
        if p >= 4:
            scopy(t, p - 4, 0).wait_recv()
            scopy(t, p - 4, 1).wait_recv()

    out_copies = [pltpu.make_async_copy(buf.at[0, p], tok_out.at[fidx[p]], osem.at[p])
                  for p in range(8)]

    def step(p):
        ready_sib(0, p)
        out_copies[p].start()
        for c in loads[p]:
            c.wait()
        d = contract(w4[p], buf[0, p])
        if p == 0:
            acc[...] = d
        else:
            acc[...] += d

    def back(p):
        ready_sib(1, p)
        dloads[p].wait()
        d = contract(wdn[p], buf[1, p])
        if p == 0:
            accb[...] = d
        else:
            accb[...] += d

    for c in inputs:
        c.wait()
    pl.semaphore_wait(barrier, len(partners))

    zcopy(0, 1).start()
    across(0, 0)
    zcopy(1, 1).start()
    zcopy(0, 2).start()
    zcopy(0, 3).start()
    pass_z(0, 1)
    pass_xy(0, 0)
    across(1, 0)
    pass_z(1, 1)
    pass_z(0, 2)
    zcopy(1, 2).start()
    pass_xy(0, 1)
    pass_d(0, 0)
    pass_z(0, 3)
    zcopy(1, 3).start()
    pass_xy(0, 2)
    pass_z(1, 2)
    pass_xy(0, 3)
    step(0)
    pass_z(1, 3)
    pass_d(0, 1)
    step(4)
    step(1)
    sib(1, 0)
    sib(2, 0)
    step(2)
    sib(3, 0)
    step(5)
    step(6)
    sib(1, 1)
    sib(2, 1)
    step(3)
    sib(3, 1)
    step(7)
    for p in (0, 4, 1, 2, 5, 6, 3, 7):
        back(p)

    chunk = hidden // 4

    def finish(k, carry):
        def part(w):
            return acc[pl.ds(pl.multiple_of(w * hidden + k * chunk, chunk), chunk)]
        r = pl.ds(pl.multiple_of(k * chunk, chunk), chunk)
        fg, fu = factors(part(0), part(1), part(2), part(3), accb[r])
        fg_out[r] = fg
        fu_out[r] = fu
        return carry
    lax.fori_loop(0, 4, finish, 0)

    for c in out_copies:
        c.wait()
    for t in (0, 1):
        for i in (1, 2, 3):
            zcopy(t, i).wait_send()
        for i in range(4):
            xcopy(t, i).wait_send()
            ycopy(t, i).wait_send()
            if t == 0:
                dxcopy(t, i).wait_send()
                dycopy(t, i).wait_send()
            else:
                dcopy(i).wait_send()
        for p in range(4):
            for h in (0, 1):
                scopy(t, p, h).wait_send()


def outer_kernel(scale, fg, fu, tok, og, ou):
    t = tok[0]
    og[...] = jnp.dot(fg[...], t, preferred_element_type=jnp.float32) * scale
    ou[...] = jnp.dot(fu[...], t, preferred_element_type=jnp.float32) * scale


def local_kernels(tokens, cotangent, w_gate, w_up, w_down, t_gate, t_up):
    n_dp, n_fs = lax.axis_size("dp"), lax.axis_size("fsdp")
    rows, cols = tokens.shape
    hidden, width = w_gate.shape
    total = rows * n_dp
    scale = 1.0 / math.sqrt(total)
    anywhere = pl.BlockSpec(memory_space=pl.ANY)
    vmem = pl.BlockSpec(memory_space=pltpu.VMEM)
    dma = pltpu.SemaphoreType.DMA
    fg, fu, tok = pl.pallas_call(
        gather_kernel,
        out_shape=(
            jax.ShapeDtypeStruct((hidden, total), jnp.bfloat16),
            jax.ShapeDtypeStruct((hidden, total), jnp.bfloat16),
            jax.ShapeDtypeStruct((n_fs, total, cols), jnp.bfloat16),
        ),
        in_specs=[anywhere] * 7,
        out_specs=(vmem, vmem, anywhere),
        scratch_shapes=[
            pltpu.VMEM((n_fs, 4 * hidden, cols), jnp.bfloat16),
            pltpu.VMEM((n_fs, hidden, cols), jnp.bfloat16),
            pltpu.VMEM((2, n_fs, total, cols), jnp.bfloat16),
            pltpu.VMEM((4 * hidden, total), jnp.float32),
            pltpu.VMEM((hidden, total), jnp.float32),
            dma((8, 4)), dma((8,)), dma((2,)), dma((8,)),
        ] + [dma((2, 4))] * 10 + [dma((2, 4, 2))] * 2,
        compiler_params=pltpu.CompilerParams(
            collective_id=0, has_side_effects=True, vmem_limit_bytes=56 * 2**20),
        cost_estimate=pl.CostEstimate(
            flops=10 * hidden * width * total, bytes_accessed=10 * hidden * width,
            transcendentals=hidden * total),
        name="gather_factors",
    )(tokens, cotangent, w_gate, w_up, t_gate, t_up, w_down)
    whole = pl.BlockSpec((hidden, total), lambda j: (0, 0))
    out = pl.BlockSpec((hidden, cols), lambda j: (0, j))
    return pl.pallas_call(
        functools.partial(outer_kernel, scale),
        grid=(n_fs,),
        out_shape=(jax.ShapeDtypeStruct((hidden, width), jnp.float32),) * 2,
        in_specs=[whole, whole, pl.BlockSpec((1, total, cols), lambda j: (j, 0, 0))],
        out_specs=(out, out),
        compiler_params=pltpu.CompilerParams(vmem_limit_bytes=60 * 2**20),
        cost_estimate=pl.CostEstimate(
            flops=4 * hidden * width * total, bytes_accessed=8 * hidden * width,
            transcendentals=0),
        name="outer",
    )(fg, fu, tok)


def local(tokens, cotangent, w_gate, w_up, w_down, t_gate, t_up):
    scale = 1.0 / math.sqrt(tokens.shape[0] * lax.axis_size("dp"))
    full_tok, full_cot = (
        lax.all_gather(lax.all_gather(a, "fsdp", axis=1, tiled=True), "dp", axis=0, tiled=True)
        for a in (tokens, cotangent)
    )
    factor_gate, factor_up = factors(
        *(contract(w, full_tok) for w in (w_gate, w_up, t_gate, t_up)),
        contract(w_down, full_cot),
    )
    return tuple(
        jnp.dot(a, full_tok, preferred_element_type=jnp.float32) * scale
        for a in (factor_gate, factor_up)
    )


def solution(mesh):
    spec = P("dp", "fsdp")
    weight = P(("dp", "fsdp"), None)
    square = mesh.shape["dp"] == 4 and mesh.shape["fsdp"] == 8
    return jax.shard_map(
        local_kernels if square else local, mesh=mesh,
        in_specs=(spec,) * 2 + (weight,) * 5, out_specs=(weight,) * 2, check_vma=False)
```

```python
import functools
import math

import jax
import jax.numpy as jnp
from jax import lax
from jax.experimental import pallas as pl
from jax.experimental.pallas import tpu as pltpu
from jax.sharding import PartitionSpec as P

MESH = pl.DeviceIdType.MESH


def contract(weight, block):
    return lax.dot_general(
        weight, block, (((1,), (1,)), ((), ())), preferred_element_type=jnp.float32
    )


def factors(gate, up, gate_dot, up_dot, back):
    s = jax.nn.sigmoid(gate)
    first = s * (1.0 + gate * (1.0 - s))
    second = s * (1.0 - s) * (2.0 + gate * (1.0 - 2.0 * s))
    factor_gate = (back * (up_dot * first + up * second * gate_dot)).astype(jnp.bfloat16)
    factor_up = (back * first * gate_dot).astype(jnp.bfloat16)
    return factor_gate, factor_up


def gather_kernel(
    tok_hbm, cot_hbm, wg, wu, tg, tu, wd,
    fg_out, fu_out, tok_out,
    w4, wdn, buf, acc, accb,
    wsem, dsem, isem, osem,
    zs, zr, xs, xr, ys, yr, dxs, dxr, dys, dyr, ss, sr,
):
    rows, cols = tok_hbm.shape
    hidden = wg.shape[0]
    half = rows // 2
    z = lax.axis_index("dp")
    f = lax.axis_index("fsdp")
    core = f % 2
    q = f // 2
    x = q % 2
    y = q // 2

    def feat(yy, xx, cc):
        return (yy * 2 + xx) * 2 + cc

    fx = feat(y, 1 - x, core)
    fy = feat(1 - y, x, core)
    fs = feat(y, x, 1 - core)
    fidx = [feat(yy, xx, cc) for cc in (core, 1 - core)
            for yy, xx in ((y, x), (y, 1 - x), (1 - y, x), (1 - y, 1 - x))]
    zi = [z, z + 1 - 2 * (z % 2), (z + 2) % 4, 3 - z]

    inputs = [pltpu.make_async_copy(src, buf.at[t, 0, pl.ds(0, rows)], isem.at[t])
              for t, src in enumerate((tok_hbm, cot_hbm))]
    for c in inputs:
        c.start()

    barrier = pltpu.get_barrier_semaphore()
    partners = [(zi[1], f), (zi[2], f), (zi[3], f), (z, fx), (z, fy), (z, fs)]
    for who in partners:
        pl.semaphore_signal(barrier, inc=1, device_id=who, device_id_type=MESH)

    loads = []
    for p in range(8):
        loads.append([
            pltpu.make_async_copy(
                src.at[:, pl.ds(pl.multiple_of(fidx[p] * cols, cols), cols)],
                w4.at[p, pl.ds(w * hidden, hidden)], wsem.at[p, w])
            for w, src in enumerate((wg, wu, tg, tu))])
    dloads = [
        pltpu.make_async_copy(
            wd.at[:, pl.ds(pl.multiple_of(fidx[p] * cols, cols), cols)],
            wdn.at[p], dsem.at[p])
        for p in range(8)]
    order = (0, 4, 1, 2, 5, 6, 3, 7)
    for p in order:
        for c in loads[p]:
            c.start()
    for p in order:
        dloads[p].start()

    def remote(t, p_src, p_dst, r_src, r_dst, n, send, recv, who):
        return pltpu.make_async_remote_copy(
            src_ref=buf.at[t, p_src, pl.ds(r_src, n)],
            dst_ref=buf.at[t, p_dst, pl.ds(r_dst, n)],
            send_sem=send, recv_sem=recv, device_id=who, device_id_type=MESH)

    def zcopy(t, i):
        return remote(t, 0, 0, 0, i * rows, rows, zs.at[t, i], zr.at[t, i], (zi[i], f))

    def xcopy(t, i):
        return remote(t, 0, 1, i * rows, i * rows, rows, xs.at[t, i], xr.at[t, i], (z, fx))

    def ycopy(t, i):
        return remote(t, 0, 2, i * rows, i * rows, rows, ys.at[t, i], yr.at[t, i], (z, fy))

    def dycopy(t, i):
        return remote(t, 1, 3, i * rows, i * rows, half, dys.at[t, i], dyr.at[t, i], (z, fy))

    def dxcopy(t, i):
        r = i * rows + half
        return remote(t, 2, 3, r, r, half, dxs.at[t, i], dxr.at[t, i], (z, fx))

    def scopy(t, p, h):
        r = h * 2 * rows
        return remote(t, p, 4 + p, r, r, 2 * rows, ss.at[t, p, h], sr.at[t, p, h], (z, fs))

    def own_xy(t):
        xcopy(t, 0).start()
        ycopy(t, 0).start()

    def pass_z(t, i):
        zcopy(t, i).wait_recv()
        xcopy(t, i).start()
        ycopy(t, i).start()
        if i % 2 == 1:
            scopy(t, 0, i // 2).start()

    def pass_xy(t, i):
        xcopy(t, i).wait_recv()
        dycopy(t, i).start()
        ycopy(t, i).wait_recv()
        dxcopy(t, i).start()
        if i % 2 == 1:
            scopy(t, 1, i // 2).start()
            scopy(t, 2, i // 2).start()

    def pass_d(t, h):
        for i in (2 * h, 2 * h + 1):
            dycopy(t, i).wait_recv()
            dxcopy(t, i).wait_recv()
        scopy(t, 3, h).start()

    def ready_sib(t, p):
        if p >= 4:
            scopy(t, p - 4, 0).wait_recv()
            scopy(t, p - 4, 1).wait_recv()

    out_copies = [pltpu.make_async_copy(buf.at[0, p], tok_out.at[fidx[p]], osem.at[p])
                  for p in range(8)]

    def step(p):
        ready_sib(0, p)
        out_copies[p].start()
        for c in loads[p]:
            c.wait()

        def body(k, carry):
            r = pl.ds(pl.multiple_of(k * hidden, hidden), hidden)
            d = contract(w4[p, r], buf[0, p])
            if p == 0:
                acc[r] = d
            else:
                acc[r] += d
            return carry
        lax.fori_loop(0, 4, body, 0)

    def back(p):
        ready_sib(1, p)
        dloads[p].wait()
        d = contract(wdn[p], buf[1, p])
        if p == 0:
            accb[...] = d
        else:
            accb[...] += d

    for c in inputs:
        c.wait()
    pl.semaphore_wait(barrier, len(partners))

    zcopy(0, 1).start()
    own_xy(0)
    zcopy(1, 1).start()
    own_xy(1)
    zcopy(0, 2).start()
    zcopy(0, 3).start()
    pass_z(0, 1)
    pass_xy(0, 0)
    pass_z(1, 1)
    pass_xy(1, 0)
    pass_z(0, 2)
    zcopy(1, 2).start()
    pass_xy(0, 1)
    pass_z(0, 3)
    zcopy(1, 3).start()
    pass_d(0, 0)
    pass_xy(1, 1)
    step(0)
    pass_z(1, 2)
    pass_xy(0, 2)
    pass_d(1, 0)
    step(4)
    pass_z(1, 3)
    pass_xy(0, 3)
    step(1)
    pass_xy(1, 2)
    step(2)
    pass_d(0, 1)
    step(5)
    pass_xy(1, 3)
    step(6)
    step(3)
    pass_d(1, 1)
    step(7)
    for p in order:
        back(p)

    chunk = hidden // 4

    def finish(k, carry):
        def part(w):
            return acc[pl.ds(pl.multiple_of(w * hidden + k * chunk, chunk), chunk)]
        r = pl.ds(pl.multiple_of(k * chunk, chunk), chunk)
        fg, fu = factors(part(0), part(1), part(2), part(3), accb[r])
        fg_out[r] = fg
        fu_out[r] = fu
        return carry
    lax.fori_loop(0, 4, finish, 0)

    for c in out_copies:
        c.wait()
    for t in (0, 1):
        for i in (1, 2, 3):
            zcopy(t, i).wait_send()
        for i in range(4):
            xcopy(t, i).wait_send()
            ycopy(t, i).wait_send()
            dxcopy(t, i).wait_send()
            dycopy(t, i).wait_send()
        for p in range(4):
            for h in (0, 1):
                scopy(t, p, h).wait_send()


def outer_kernel(scale, fg, fu, tok, og, ou):
    t = tok[0]
    og[...] = jnp.dot(fg[...], t, preferred_element_type=jnp.float32) * scale
    ou[...] = jnp.dot(fu[...], t, preferred_element_type=jnp.float32) * scale


def local_kernels(tokens, cotangent, w_gate, w_up, w_down, t_gate, t_up):
    n_dp, n_fs = lax.axis_size("dp"), lax.axis_size("fsdp")
    rows, cols = tokens.shape
    hidden, width = w_gate.shape
    total = rows * n_dp
    scale = 1.0 / math.sqrt(total)
    anywhere = pl.BlockSpec(memory_space=pl.ANY)
    vmem = pl.BlockSpec(memory_space=pltpu.VMEM)
    dma = pltpu.SemaphoreType.DMA
    fg, fu, tok = pl.pallas_call(
        gather_kernel,
        out_shape=(
            jax.ShapeDtypeStruct((hidden, total), jnp.bfloat16),
            jax.ShapeDtypeStruct((hidden, total), jnp.bfloat16),
            jax.ShapeDtypeStruct((n_fs, total, cols), jnp.bfloat16),
        ),
        in_specs=[anywhere] * 7,
        out_specs=(vmem, vmem, anywhere),
        scratch_shapes=[
            pltpu.VMEM((n_fs, 4 * hidden, cols), jnp.bfloat16),
            pltpu.VMEM((n_fs, hidden, cols), jnp.bfloat16),
            pltpu.VMEM((2, n_fs, total, cols), jnp.bfloat16),
            pltpu.VMEM((4 * hidden, total), jnp.float32),
            pltpu.VMEM((hidden, total), jnp.float32),
            dma((8, 4)), dma((8,)), dma((2,)), dma((8,)),
        ] + [dma((2, 4))] * 10 + [dma((2, 4, 2))] * 2,
        compiler_params=pltpu.CompilerParams(
            collective_id=0, has_side_effects=True, vmem_limit_bytes=56 * 2**20),
        cost_estimate=pl.CostEstimate(
            flops=10 * hidden * width * total, bytes_accessed=10 * hidden * width,
            transcendentals=hidden * total),
        name="gather_factors",
    )(tokens, cotangent, w_gate, w_up, t_gate, t_up, w_down)
    whole = pl.BlockSpec((hidden, total), lambda j: (0, 0))
    out = pl.BlockSpec((hidden, cols), lambda j: (0, j))
    return pl.pallas_call(
        functools.partial(outer_kernel, scale),
        grid=(n_fs,),
        out_shape=(jax.ShapeDtypeStruct((hidden, width), jnp.float32),) * 2,
        in_specs=[whole, whole, pl.BlockSpec((1, total, cols), lambda j: (j, 0, 0))],
        out_specs=(out, out),
        compiler_params=pltpu.CompilerParams(vmem_limit_bytes=60 * 2**20),
        cost_estimate=pl.CostEstimate(
            flops=4 * hidden * width * total, bytes_accessed=8 * hidden * width,
            transcendentals=0),
        name="outer",
    )(fg, fu, tok)


def local(tokens, cotangent, w_gate, w_up, w_down, t_gate, t_up):
    scale = 1.0 / math.sqrt(tokens.shape[0] * lax.axis_size("dp"))
    full_tok, full_cot = (
        lax.all_gather(lax.all_gather(a, "fsdp", axis=1, tiled=True), "dp", axis=0, tiled=True)
        for a in (tokens, cotangent)
    )
    factor_gate, factor_up = factors(
        *(contract(w, full_tok) for w in (w_gate, w_up, t_gate, t_up)),
        contract(w_down, full_cot),
    )
    return tuple(
        jnp.dot(a, full_tok, preferred_element_type=jnp.float32) * scale
        for a in (factor_gate, factor_up)
    )


def solution(mesh):
    spec = P("dp", "fsdp")
    weight = P(("dp", "fsdp"), None)
    square = mesh.shape["dp"] == 4 and mesh.shape["fsdp"] == 8
    return jax.shard_map(
        local_kernels if square else local, mesh=mesh,
        in_specs=(spec,) * 2 + (weight,) * 5, out_specs=(weight,) * 2, check_vma=False)
```
